256 devices in a mesh: role: 4 (over z_hi), dp: 8 (over x, core), mp: 8 (over y, z_lo).
Axes of the slice: x: 4, y: 4, z: 8 (z_hi: 4, z_lo: 2; z = z_hi * 2 + z_lo), core: 2. Of those that a mesh axis runs over, the one named last changes fastest.
Arguments:
- teacher_hidden: bfloat16 [8192, 2560], P('dp', ('role', 'mp')), may hold values from -20 to 20
- teacher_gain: float32 [2560], replicated, may hold values from 0.25 to 1.75
- teacher_head: bfloat16 [2560, 3, 8192], P(None, None, ('role', 'mp')), may hold values from -4.1504894 to 4.1504894
- student_hidden: bfloat16 [8192, 1024], P('dp', ('role', 'mp')), may hold values from -20 to 20
- norm_gain: float32 [1024], replicated, may hold values from 0.25 to 1.75
- gate_weight: bfloat16 [1024, 4096], P(None, ('role', 'mp')), may hold values from -0.1875 to 0.1875
- up_weight: bfloat16 [1024, 4096], P(None, ('role', 'mp')), may hold values from -0.1875 to 0.1875
- down_weight: bfloat16 [4096, 1024], P(('role', 'mp')), may hold values from -0.09375 to 0.09375
- final_gain: float32 [1024], replicated, may hold values from 0.25 to 1.75
- student_head: bfloat16 [1024, 3, 8192], P(None, None, ('role', 'mp')), may hold values from -6.5625 to 6.5625
- sampled_codes: int32 [8192], P('dp'), may hold values from 0 to 8191
- levels: int32 [8192], P('dp'), may hold values from 0 to 2
Outputs:
- token_kl: float32 [8192], P('dp')
- sampled_score: float32 [8192], P('dp')
- head_grad: float32 [1024, 3, 8192], P('dp', None, ('role', 'mp'))
- gate_grad: float32 [1024, 4096], P('dp', ('role', 'mp'))
- up_grad: float32 [1024, 4096], P('dp', ('role', 'mp'))
- down_grad: float32 [4096, 1024], P(('role', 'mp'), 'dp')
- input_grad: float32 [8192, 1024], P('dp', ('role', 'mp'))
The draws below stay inside these ranges and needn't reach their ends.
All inputs are finite; a program needn't handle non-finite values.
Results may differ from the reference program's by a relative error of at most 0.035.
Values may be sent and summed in bfloat16 or wider, within the bound.
No kernel may reach another device: no remote copies, remote signals or barrier semaphores. Data moves between devices by JAX's collectives and lax.ppermute only.
A program may use at most 128 MiB of HBM per device.

```python
import math
import jax
import jax.numpy as jnp
from jax import lax

DT = 2560
DS = 1024
FS = 4096
CODES = 8192
LEVELS = 3
TOKENS = 8192


def head_values(key, salt, width):
    normal_draw = jax.random.normal(jax.random.fold_in(key, salt), (width, LEVELS, CODES), jnp.float32)
    common_draw = jax.random.normal(jax.random.fold_in(key, salt + 100), (width, LEVELS, 1), jnp.float32)
    return (jnp.clip(normal_draw, -5.0, 5.0) * 5.0 + jnp.clip(common_draw, -3.0, 3.0) * 60.0) / math.sqrt(width)


def level_values(key):
    return jax.random.randint(jax.random.fold_in(key, 41), (TOKENS,), 0, LEVELS, dtype=jnp.int32)


def hidden_rows(key, width):
    return jnp.clip(jax.random.normal(key, (TOKENS, width), jnp.float32), -5.0, 5.0)


def draw_teacher_head(key, part):
    return head_values(key, 11, DT).astype(jnp.bfloat16)


def draw_student_head(key, part):
    return head_values(key, 13, DS).astype(jnp.bfloat16)


def draw_levels(key, part):
    return level_values(key)


def draw_teacher_hidden(key, part):
    key = jax.random.fold_in(key, 3)
    return hidden_rows(key, DT).astype(jnp.bfloat16)


def draw_student_hidden(key, part):
    key = jax.random.fold_in(key, 7)
    return hidden_rows(key, DS).astype(jnp.bfloat16)


def with_ends(values, rng, least, high):
    extent = values.shape
    spot = [jax.random.randint(jax.random.fold_in(rng, axis), (), 0, extent[axis]) for axis in range(len(extent))]
    values = values.at[tuple(spot)].set(least)
    longest = extent.index(max(extent))
    spot[longest] = (spot[longest] + 1) % extent[longest]
    return values.at[tuple(spot)].set(high)


def block_scale(key, shape, pieces, low, high):
    factor_of, own = 1.0, jax.random.fold_in(key, 6)
    for position, blocks in pieces:
        heights = jnp.exp(jax.random.uniform(jax.random.fold_in(own, position), (blocks,), jnp.float32, low / len(pieces), high / len(pieces)))
        factor_of = factor_of * jnp.repeat(heights, shape[position] // blocks).reshape([-1 if axis == position else 1 for axis in range(len(shape))])
    return factor_of


def centred(rng, dims, deviation, most, cuts=(), kind=jnp.bfloat16):
    loudness = block_scale(rng, dims, cuts, -0.22, 0.18) if cuts else 1.0
    array = jax.random.normal(rng, dims, jnp.float32) * deviation * loudness
    return jnp.minimum(jnp.maximum(array, -most), most).astype(kind)


def setup_inputs(seed: int = 0) -> dict:
    key_of = jax.random.split(jax.random.key(seed), 13)
    teacher_hidden = draw_teacher_hidden(jax.random.fold_in(key_of[12], 71), 0)
    teacher_gain = jnp.clip(1.0 + 0.15 * jax.random.normal(key_of[1], (DT,), jnp.float32), 0.25, 1.75)
    teacher_head = draw_teacher_head(jax.random.fold_in(key_of[12], 71), 0)
    student_hidden = draw_student_hidden(jax.random.fold_in(key_of[12], 71), 0)
    norm_gain = jnp.clip(1.0 + 0.15 * jax.random.normal(key_of[4], (DS,), jnp.float32), 0.25, 1.75)
    gate_weight = centred(key_of[5], (DS, FS), DS ** -0.5, 0.1875, ((1, 32),))
    up_weight = centred(key_of[6], (DS, FS), DS ** -0.5, 0.1875, ((1, 32),))
    down_weight = centred(key_of[7], (FS, DS), FS ** -0.5, 0.09375, ((0, 32),))
    final_gain = jnp.clip(1.0 + 0.15 * jax.random.normal(key_of[8], (DS,), jnp.float32), 0.25, 1.75)
    student_head = draw_student_head(jax.random.fold_in(key_of[12], 71), 0)
    sampled_codes = with_ends(jax.random.randint(key_of[10], (TOKENS,), 0, CODES), jax.random.fold_in(key_of[10], 1), 0, CODES - 1).astype(jnp.int32)
    levels = draw_levels(jax.random.fold_in(key_of[12], 71), 0)
    return dict(teacher_hidden=teacher_hidden, teacher_gain=teacher_gain, teacher_head=teacher_head, student_hidden=student_hidden, norm_gain=norm_gain, gate_weight=gate_weight, up_weight=up_weight, down_weight=down_weight, final_gain=final_gain, student_head=student_head, sampled_codes=sampled_codes, levels=levels)


NORM_EPS = 1e-06

def rms_scale(values):
    return lax.rsqrt(lax.optimization_barrier(jnp.mean(values * values, axis=1)) + NORM_EPS)

def silu_parts(gate_pre):
    sigma = jax.nn.sigmoid(gate_pre)
    return (gate_pre * sigma, sigma * (1.0 + gate_pre * (1.0 - sigma)))

def reference(teacher_hidden, teacher_gain, teacher_head, student_hidden, norm_gain, gate_weight, up_weight, down_weight, final_gain, student_head, sampled_codes, levels):
    level_mask = (levels[:, None] == jnp.arange(LEVELS, dtype=jnp.int32)[None, :]).astype(jnp.float32)
    teacher_wide = teacher_hidden.astype(jnp.float32)
    teacher_normed = (teacher_wide * rms_scale(teacher_wide)[:, None] * teacher_gain).astype(jnp.bfloat16)
    student_in = student_hidden.astype(jnp.float32)
    scale_in = rms_scale(student_in)
    normed_in = (student_in * scale_in[:, None] * norm_gain).astype(jnp.bfloat16)
    gate_pre = jnp.dot(normed_in, gate_weight, preferred_element_type=jnp.float32)
    up_pre = jnp.dot(normed_in, up_weight, preferred_element_type=jnp.float32)
    gate_act, gate_slope = silu_parts(gate_pre)
    hidden = (gate_act * up_pre).astype(jnp.bfloat16)
    mixed_rows = student_in + jnp.dot(hidden, down_weight, preferred_element_type=jnp.float32)
    scale_out = rms_scale(mixed_rows)
    normed_out = (mixed_rows * scale_out[:, None] * final_gain).astype(jnp.bfloat16)
    teacher_logits = jnp.zeros((TOKENS, CODES), jnp.float32)
    student_logits = jnp.zeros((TOKENS, CODES), jnp.float32)
    for level_idx in range(LEVELS):
        pick = level_mask[:, level_idx, None]
        teacher_logits = teacher_logits + pick * jnp.dot(teacher_normed, teacher_head[:, level_idx, :], preferred_element_type=jnp.float32)
        student_logits = student_logits + pick * jnp.dot(normed_out, student_head[:, level_idx, :], preferred_element_type=jnp.float32)
    teacher_log = teacher_logits - jax.nn.logsumexp(teacher_logits, axis=1, keepdims=True)
    student_log = student_logits - jax.nn.logsumexp(student_logits, axis=1, keepdims=True)
    teacher_prob = jnp.exp(teacher_log)
    token_kl = lax.optimization_barrier(jnp.sum(teacher_prob * (teacher_log - student_log), axis=1))
    sampled_score = jnp.take_along_axis(teacher_log, sampled_codes[:, None].astype(jnp.int32), axis=1)[:, 0]
    code_grad = jnp.exp(student_log) - teacher_prob
    head_parts = []
    back_out = jnp.zeros((TOKENS, DS), jnp.float32)
    for level_idx in range(LEVELS):
        level_grad = (level_mask[:, level_idx, None] * code_grad).astype(jnp.bfloat16)
        head_parts.append(jnp.dot(normed_out.T, level_grad, preferred_element_type=jnp.float32))
        back_out = back_out + jnp.dot(level_grad, student_head[:, level_idx, :].T, preferred_element_type=jnp.float32)
    head_grad = jnp.stack(head_parts, axis=1)
    gained = final_gain * back_out
    back_mixed = scale_out[:, None] * gained - mixed_rows * (scale_out ** 3)[:, None] * lax.optimization_barrier(jnp.mean(gained * mixed_rows, axis=1))[:, None]
    back_mixed_b = back_mixed.astype(jnp.bfloat16)
    back_hidden = jnp.dot(back_mixed_b, down_weight.T, preferred_element_type=jnp.float32)
    back_gate = (back_hidden * up_pre * gate_slope).astype(jnp.bfloat16)
    back_up = (back_hidden * gate_act).astype(jnp.bfloat16)
    gate_grad = jnp.dot(normed_in.T, back_gate, preferred_element_type=jnp.float32)
    up_grad = jnp.dot(normed_in.T, back_up, preferred_element_type=jnp.float32)
    down_grad = jnp.dot(hidden.T, back_mixed_b, preferred_element_type=jnp.float32)
    back_in = jnp.dot(back_gate, gate_weight.T, preferred_element_type=jnp.float32) + jnp.dot(back_up, up_weight.T, preferred_element_type=jnp.float32)
    gained_in = norm_gain * back_in
    input_grad = back_mixed + scale_in[:, None] * gained_in - student_in * (scale_in ** 3)[:, None] * lax.optimization_barrier(jnp.mean(gained_in * student_in, axis=1))[:, None]
    return (token_kl, sampled_score, head_grad, gate_grad, up_grad, down_grad, input_grad)
```

```python
import jax
import jax.numpy as jnp
from jax import lax
from jax.sharding import Mesh, PartitionSpec as P

NORM_EPS = 1e-06
OUTER = "zh"
INNER = ("y", "zl")
GROUP = ("zh", "y", "zl")
ROWS = ("x", "core")
F32 = jnp.float32
BF16 = jnp.bfloat16


def dot(a, b, da, db):
    return lax.dot_general(a, b, (((da,), (db,)), ((), ())), preferred_element_type=F32)


def spread(block, axes, count):
    copies = jnp.broadcast_to(block[None], (count,) + block.shape)
    got = lax.all_to_all(copies, axes, 0, 0, tiled=True)
    return got.reshape((count * block.shape[0],) + block.shape[1:])


def collect(terms, axes, count):
    parts = terms.reshape((count, terms.shape[0] // count) + terms.shape[1:])
    got = lax.all_to_all(parts, axes, 0, 0, tiled=True)
    return jnp.sum(got.astype(F32), axis=0)


def body(
    teacher_hidden,
    teacher_gain,
    teacher_head,
    student_hidden,
    norm_gain,
    gate_weight,
    up_weight,
    down_weight,
    final_gain,
    student_head,
    sampled_codes,
    levels,
):
    outer, inner, dp = 4, 8, 8
    row_count = teacher_hidden.shape[0]
    level_count = teacher_head.shape[1]
    code_count = teacher_head.shape[2]
    width_t = teacher_gain.shape[0]
    width_s = norm_gain.shape[0]
    share = student_hidden.shape[1]
    outer_at = lax.axis_index(OUTER)
    inner_at = lax.axis_index(INNER)
    group_at = outer_at * inner + inner_at

    def to_gathered(w):
        return jnp.swapaxes(w.reshape((outer, inner, -1) + w.shape[1:]), 0, 1).reshape(w.shape)

    def from_gathered(w):
        return jnp.swapaxes(w.reshape((inner, outer, -1) + w.shape[1:]), 0, 1).reshape(w.shape)

    teacher_flat = teacher_head.reshape(width_t, level_count * code_count)
    student_flat = student_head.reshape(width_s, level_count * code_count)
    level_mask = (jnp.arange(level_count, dtype=jnp.int32)[:, None] == levels[None, :]).astype(F32)

    teacher_t = lax.all_gather(teacher_hidden.T, OUTER, axis=0, tiled=True)
    teacher_t = lax.all_gather(teacher_t, INNER, axis=0, tiled=True)

    own_cols = student_hidden.T
    student_t = spread(spread(own_cols, OUTER, outer), INNER, inner)
    student_in = student_t.astype(F32)
    scale_in = lax.rsqrt(jnp.mean(student_in * student_in, axis=0) + NORM_EPS)
    gain_in = to_gathered(norm_gain)
    normed_in = (student_in * scale_in[None, :] * gain_in[:, None]).astype(BF16)
    both_weight = to_gathered(jnp.concatenate([gate_weight, up_weight], axis=1))
    both_pre = dot(both_weight, normed_in, 0, 0)
    units = gate_weight.shape[1]
    gate_pre, up_pre = both_pre[:units], both_pre[units:]
    sigma = jax.nn.sigmoid(gate_pre)
    gate_act = gate_pre * sigma
    gate_slope = sigma * (1.0 + gate_pre * (1.0 - sigma))
    hidden = (gate_act * up_pre).astype(BF16)
    down_part = dot(hidden, down_weight, 0, 0).astype(BF16)
    down_own = collect(collect(down_part, INNER, inner).astype(BF16), OUTER, outer)
    own_rows = row_count // (outer * inner)
    row_start = (inner_at * outer + outer_at) * own_rows
    student_own = lax.dynamic_slice_in_dim(student_t, row_start, own_rows, 1).astype(F32)
    mixed_rows = from_gathered(student_own).T + down_own
    scale_out = lax.rsqrt(jnp.mean(mixed_rows * mixed_rows, axis=1) + NORM_EPS)
    normed_own = (mixed_rows * scale_out[:, None] * final_gain).astype(BF16)
    normed_out = spread(spread(normed_own, OUTER, outer), INNER, inner)

    teacher_wide = from_gathered(teacher_t).astype(F32)
    teacher_scale = lax.rsqrt(jnp.mean(teacher_wide * teacher_wide, axis=0) + NORM_EPS)
    teacher_normed = (teacher_wide * teacher_scale[None, :] * teacher_gain[:, None]).astype(BF16)

    def pick_level(all_levels):
        return jnp.sum(
            all_levels.reshape(level_count, code_count, row_count) * level_mask[:, None, :], axis=0
        )

    teacher_logits = pick_level(dot(teacher_flat, teacher_normed, 0, 0))
    student_logits = pick_level(dot(student_flat, normed_out, 0, 1))
    peak_s = jnp.max(student_logits, axis=0)
    peak_t = jnp.max(teacher_logits, axis=0)
    expo_t = jnp.exp(teacher_logits - peak_t)
    total_t = jnp.sum(expo_t, axis=0)
    part_s = peak_s + jnp.log(jnp.sum(jnp.exp(student_logits - peak_s), axis=0))
    part_t = peak_t + jnp.log(total_t)
    part_cross = jnp.sum(expo_t * (teacher_logits - student_logits), axis=0) / total_t
    codes_here = group_at * code_count + jnp.arange(code_count, dtype=jnp.int32)
    part_score = jnp.sum(
        jnp.where(codes_here[:, None] == sampled_codes[None, :], teacher_logits, 0.0), axis=0
    )
    stats = jnp.stack([part_s, part_t, part_cross, part_score])
    stats = spread(stats, GROUP, outer * inner).reshape(outer * inner, 4, row_count)
    norm_s = jax.nn.logsumexp(stats[:, 0], axis=0)
    norm_t = jax.nn.logsumexp(stats[:, 1], axis=0)
    cross = jnp.sum(jnp.exp(stats[:, 1] - norm_t) * stats[:, 2], axis=0)
    token_kl = cross - norm_t + norm_s
    sampled_score = jnp.sum(stats[:, 3], axis=0) - norm_t
    code_grad = jnp.exp(student_logits - norm_s) - jnp.exp(teacher_logits - norm_t)
    grad_full = (
        (level_mask[:, None, :] * code_grad[None])
        .astype(BF16)
        .reshape(level_count * code_count, row_count)
    )

    code_part = dot(grad_full, student_flat, 0, 1)
    back_out = collect(collect(code_part, INNER, inner), OUTER, outer)
    head_term = dot(normed_out, grad_full, 0, 1).astype(BF16)
    head_share = lax.psum_scatter(head_term, ROWS, scatter_dimension=0, tiled=True).astype(F32)
    gained = final_gain * back_out
    back_mixed = (
        scale_out[:, None] * gained
        - mixed_rows * (scale_out**3)[:, None] * jnp.mean(gained * mixed_rows, axis=1)[:, None]
    )
    back_mixed_b = spread(spread(back_mixed.astype(BF16), OUTER, outer), INNER, inner)

    back_hidden = dot(down_weight, back_mixed_b, 1, 1)
    back_both = jnp.concatenate(
        [
            (back_hidden * up_pre * gate_slope).astype(BF16),
            (back_hidden * gate_act).astype(BF16),
        ]
    )
    both_term = from_gathered(dot(normed_in, back_both, 1, 1).astype(BF16))
    down_term = dot(back_mixed_b, hidden, 0, 1).astype(BF16)
    grad_share = lax.psum_scatter(
        jnp.concatenate([both_term, down_term], axis=1), ROWS, scatter_dimension=0, tiled=True
    ).astype(F32)
    gate_share = grad_share[:, :units]
    up_share = grad_share[:, units : 2 * units]
    down_share = grad_share[:, 2 * units :].T

    back_part = dot(both_weight, back_both, 1, 0)
    row_part = jnp.sum(gain_in[:, None] * student_in * back_part, axis=0)

    def with_rows(part, row_term, count):
        high = row_term.astype(BF16)
        low = (row_term - high.astype(F32)).astype(BF16)
        extra = jnp.concatenate(
            [high[None], low[None], jnp.zeros((14, row_count), BF16)], axis=0
        )
        part = part.astype(BF16).reshape(count, -1, row_count)
        extra = jnp.broadcast_to(extra[None], (count, 16, row_count))
        return jnp.concatenate([part, extra], axis=1).reshape(-1, row_count)

    got = collect(with_rows(back_part, row_part, inner), INNER, inner)
    block = outer * share
    got = collect(with_rows(got[:block], got[block] + got[block + 1], outer), OUTER, outer)
    back_in = got[:share]
    row_mean = (got[share] + got[share + 1]) / width_s
    share_start = group_at * share
    back_own = lax.dynamic_slice_in_dim(back_mixed_b, share_start, share, 1).T.astype(F32)
    own_gain = lax.dynamic_slice_in_dim(norm_gain, share_start, share, 0)
    input_grad = (
        back_own
        + scale_in * own_gain[:, None] * back_in
        - own_cols.astype(F32) * (scale_in**3 * row_mean)
    ).T
    head_grad = head_share.reshape(head_share.shape[0], level_count, code_count)
    return (token_kl, sampled_score, head_grad, gate_share, up_share, down_share, input_grad)


def solution(mesh):
    split = Mesh(mesh.devices.reshape(4, 4, 2, 4, 2), ("zh", "x", "core", "y", "zl"))
    placed = (
        P(ROWS, GROUP),
        P(),
        P(None, None, GROUP),
        P(ROWS, GROUP),
        P(),
        P(None, GROUP),
        P(None, GROUP),
        P(GROUP, None),
        P(),
        P(None, None, GROUP),
        P(ROWS),
        P(ROWS),
    )
    return jax.shard_map(
        body,
        mesh=split,
        in_specs=placed,
        out_specs=(
            P(ROWS),
            P(ROWS),
            P(ROWS, None, GROUP),
            P(ROWS, GROUP),
            P(ROWS, GROUP),
            P(GROUP, ROWS),
            P(ROWS, GROUP),
        ),
        check_vma=False,
    )
```

```python
import jax
import jax.numpy as jnp
from jax import lax
from jax.sharding import Mesh, PartitionSpec as P

NORM_EPS = 1e-06
OUTER = "zh"
INNER = ("y", "zl")
GROUP = ("zh", "y", "zl")
ROWS = ("x", "core")
F32 = jnp.float32
BF16 = jnp.bfloat16


def dot(a, b, da, db):
    return lax.dot_general(a, b, (((da,), (db,)), ((), ())), preferred_element_type=F32)


def spread(block, axes, count):
    copies = jnp.broadcast_to(block[None], (count,) + block.shape)
    got = lax.all_to_all(copies, axes, 0, 0, tiled=True)
    return got.reshape((count * block.shape[0],) + block.shape[1:])


def collect(terms, axes, count):
    parts = terms.reshape((count, terms.shape[0] // count) + terms.shape[1:])
    got = lax.all_to_all(parts, axes, 0, 0, tiled=True)
    return jnp.sum(got.astype(F32), axis=0)


def body(
    teacher_hidden,
    teacher_gain,
    teacher_head,
    student_hidden,
    norm_gain,
    gate_weight,
    up_weight,
    down_weight,
    final_gain,
    student_head,
    sampled_codes,
    levels,
):
    outer, inner, dp = 4, 8, 8
    row_count = teacher_hidden.shape[0]
    level_count = teacher_head.shape[1]
    code_count = teacher_head.shape[2]
    width_t = teacher_gain.shape[0]
    width_s = norm_gain.shape[0]
    share = student_hidden.shape[1]
    outer_at = lax.axis_index(OUTER)
    inner_at = lax.axis_index(INNER)
    group_at = outer_at * inner + inner_at

    def to_gathered(w):
        return jnp.swapaxes(w.reshape((outer, inner, -1) + w.shape[1:]), 0, 1).reshape(w.shape)

    def from_gathered(w):
        return jnp.swapaxes(w.reshape((inner, outer, -1) + w.shape[1:]), 0, 1).reshape(w.shape)

    teacher_flat = teacher_head.reshape(width_t, level_count * code_count)
    student_flat = student_head.reshape(width_s, level_count * code_count)
    level_mask = (jnp.arange(level_count, dtype=jnp.int32)[:, None] == levels[None, :]).astype(F32)

    teacher_t = spread(spread(teacher_hidden.T, OUTER, outer), INNER, inner)

    own_cols = student_hidden.T
    student_t = spread(spread(own_cols, OUTER, outer), INNER, inner)
    student_in = student_t.astype(F32)
    scale_in = lax.rsqrt(jnp.mean(student_in * student_in, axis=0) + NORM_EPS)
    gain_in = to_gathered(norm_gain)
    normed_in = (student_in * scale_in[None, :] * gain_in[:, None]).astype(BF16)
    both_weight = to_gathered(jnp.concatenate([gate_weight, up_weight], axis=1))
    both_pre = dot(both_weight, normed_in, 0, 0)
    units = gate_weight.shape[1]
    gate_pre, up_pre = both_pre[:units], both_pre[units:]
    sigma = jax.nn.sigmoid(gate_pre)
    gate_act = gate_pre * sigma
    gate_slope = sigma * (1.0 + gate_pre * (1.0 - sigma))
    hidden = (gate_act * up_pre).astype(BF16)
    down_part = dot(hidden, down_weight, 0, 0).astype(BF16)
    down_own = collect(collect(down_part, INNER, inner).astype(BF16), OUTER, outer)
    own_rows = row_count // (outer * inner)
    row_start = (inner_at * outer + outer_at) * own_rows
    student_own = lax.dynamic_slice_in_dim(student_t, row_start, own_rows, 1).astype(F32)
    mixed_rows = from_gathered(student_own).T + down_own
    scale_out = lax.rsqrt(jnp.mean(mixed_rows * mixed_rows, axis=1) + NORM_EPS)
    normed_own = (mixed_rows * scale_out[:, None] * final_gain).astype(BF16)

    centre_part = jnp.mean(student_head.astype(F32), axis=2).T
    centre_part = jnp.pad(centre_part, ((0, 16 - level_count), (0, 0)))
    sent = spread(jnp.concatenate([normed_own, centre_part.astype(BF16)]), OUTER, outer)
    sent = sent.reshape(outer, -1, width_s)
    centre_part = jnp.mean(sent[:, own_rows:].astype(F32), axis=0)
    sent = jnp.concatenate(
        [sent[:, :own_rows].reshape(-1, width_s), centre_part.astype(BF16)], axis=0
    )
    sent = spread(sent, INNER, inner).reshape(inner, -1, width_s)
    normed_out = sent[:, : outer * own_rows].reshape(row_count, width_s)
    centre = jnp.mean(sent[:, outer * own_rows :].astype(F32), axis=0)[:level_count]
    student_centred = (
        (student_head.astype(F32) - centre.T[:, :, None])
        .astype(BF16)
        .reshape(width_s, level_count * code_count)
    )

    teacher_wide = from_gathered(teacher_t).astype(F32)
    teacher_scale = lax.rsqrt(jnp.mean(teacher_wide * teacher_wide, axis=0) + NORM_EPS)
    teacher_normed = (teacher_wide * teacher_scale[None, :] * teacher_gain[:, None]).astype(BF16)

    def pick_level(all_levels):
        return jnp.sum(
            all_levels.reshape(level_count, code_count, row_count) * level_mask[:, None, :], axis=0
        )

    teacher_logits = pick_level(dot(teacher_flat, teacher_normed, 0, 0))
    student_logits = pick_level(dot(student_flat, normed_out, 0, 1))
    peak_s = jnp.max(student_logits, axis=0)
    peak_t = jnp.max(teacher_logits, axis=0)
    expo_t = jnp.exp(teacher_logits - peak_t)
    total_t = jnp.sum(expo_t, axis=0)
    part_s = peak_s + jnp.log(jnp.sum(jnp.exp(student_logits - peak_s), axis=0))
    part_t = peak_t + jnp.log(total_t)
    part_cross = jnp.sum(expo_t * (teacher_logits - student_logits), axis=0) / total_t
    codes_here = group_at * code_count + jnp.arange(code_count, dtype=jnp.int32)
    part_score = jnp.sum(
        jnp.where(codes_here[:, None] == sampled_codes[None, :], teacher_logits, 0.0), axis=0
    )
    stats = jnp.stack([part_s, part_t, part_cross, part_score])
    stats = spread(stats, GROUP, outer * inner).reshape(outer * inner, 4, row_count)
    norm_s = jax.nn.logsumexp(stats[:, 0], axis=0)
    norm_t = jax.nn.logsumexp(stats[:, 1], axis=0)
    cross = jnp.sum(jnp.exp(stats[:, 1] - norm_t) * stats[:, 2], axis=0)
    token_kl = cross - norm_t + norm_s
    sampled_score = jnp.sum(stats[:, 3], axis=0) - norm_t
    code_grad = jnp.exp(student_logits - norm_s) - jnp.exp(teacher_logits - norm_t)
    grad_full = (
        (level_mask[:, None, :] * code_grad[None])
        .astype(BF16)
        .reshape(level_count * code_count, row_count)
    )

    code_part = dot(grad_full, student_centred, 0, 1).astype(BF16)
    back_out = collect(collect(code_part, INNER, inner).astype(BF16), OUTER, outer)
    head_term = dot(normed_out, grad_full, 0, 1).astype(BF16)
    head_share = collect(head_term, ROWS, dp)
    gained = final_gain * back_out
    back_mixed = (
        scale_out[:, None] * gained
        - mixed_rows * (scale_out**3)[:, None] * jnp.mean(gained * mixed_rows, axis=1)[:, None]
    )
    back_mixed_b = spread(spread(back_mixed.astype(BF16), OUTER, outer), INNER, inner)

    back_hidden = dot(down_weight, back_mixed_b, 1, 1)
    back_both = jnp.concatenate(
        [
            (back_hidden * up_pre * gate_slope).astype(BF16),
            (back_hidden * gate_act).astype(BF16),
        ]
    )
    both_term = from_gathered(dot(normed_in, back_both, 1, 1).astype(BF16))
    down_term = dot(back_mixed_b, hidden, 0, 1).astype(BF16)
    grad_share = collect(jnp.concatenate([both_term, down_term], axis=1), ROWS, dp)
    gate_share = grad_share[:, :units]
    up_share = grad_share[:, units : 2 * units]
    down_share = grad_share[:, 2 * units :].T

    back_part = dot(both_weight, back_both, 1, 0)
    row_part = jnp.sum(gain_in[:, None] * student_in * back_part, axis=0)

    def with_rows(part, row_term, count):
        high = row_term.astype(BF16)
        low = (row_term - high.astype(F32)).astype(BF16)
        extra = jnp.concatenate(
            [high[None], low[None], jnp.zeros((14, row_count), BF16)], axis=0
        )
        part = part.astype(BF16).reshape(count, -1, row_count)
        extra = jnp.broadcast_to(extra[None], (count, 16, row_count))
        return jnp.concatenate([part, extra], axis=1).reshape(-1, row_count)

    got = collect(with_rows(back_part, row_part, inner), INNER, inner)
    block = outer * share
    got = collect(with_rows(got[:block], got[block] + got[block + 1], outer), OUTER, outer)
    back_in = got[:share]
    row_mean = (got[share] + got[share + 1]) / width_s
    share_start = group_at * share
    back_own = lax.dynamic_slice_in_dim(back_mixed_b, share_start, share, 1).T.astype(F32)
    own_gain = lax.dynamic_slice_in_dim(norm_gain, share_start, share, 0)
    input_grad = (
        back_own
        + scale_in * own_gain[:, None] * back_in
        - own_cols.astype(F32) * (scale_in**3 * row_mean)
    ).T
    head_grad = head_share.reshape(head_share.shape[0], level_count, code_count)
    return (token_kl, sampled_score, head_grad, gate_share, up_share, down_share, input_grad)


def solution(mesh):
    split = Mesh(mesh.devices.reshape(4, 4, 2, 4, 2), ("zh", "x", "core", "y", "zl"))
    placed = (
        P(ROWS, GROUP),
        P(),
        P(None, None, GROUP),
        P(ROWS, GROUP),
        P(),
        P(None, GROUP),
        P(None, GROUP),
        P(GROUP, None),
        P(),
        P(None, None, GROUP),
        P(ROWS),
        P(ROWS),
    )
    return jax.shard_map(
        body,
        mesh=split,
        in_specs=placed,
        out_specs=(
            P(ROWS),
            P(ROWS),
            P(ROWS, None, GROUP),
            P(ROWS, GROUP),
            P(ROWS, GROUP),
            P(GROUP, ROWS),
            P(ROWS, GROUP),
        ),
        check_vma=False,
    )
```

```python
import jax
import jax.numpy as jnp
from jax import lax
from jax.sharding import Mesh, PartitionSpec as P

NORM_EPS = 1e-06
OUTER = ("zh", "zl")
INNER = "y"
GROUP = ("zh", "y", "zl")
ROWS = ("x", "core")
F32 = jnp.float32
BF16 = jnp.bfloat16


def dot(a, b, da, db):
    return lax.dot_general(a, b, (((da,), (db,)), ((), ())), preferred_element_type=F32)


def spread(block, axes, count):
    copies = jnp.broadcast_to(block[None], (count,) + block.shape)
    got = lax.all_to_all(copies, axes, 0, 0, tiled=True)
    return got.reshape((count * block.shape[0],) + block.shape[1:])


def collect(terms, axes, count):
    parts = terms.reshape((count, terms.shape[0] // count) + terms.shape[1:])
    got = lax.all_to_all(parts, axes, 0, 0, tiled=True)
    return jnp.sum(got.astype(F32), axis=0)


def body(
    teacher_hidden,
    teacher_gain,
    teacher_head,
    student_hidden,
    norm_gain,
    gate_weight,
    up_weight,
    down_weight,
    final_gain,
    student_head,
    sampled_codes,
    levels,
):
    outer, inner, dp = 8, 4, 8
    row_count = teacher_hidden.shape[0]
    level_count = teacher_head.shape[1]
    code_count = teacher_head.shape[2]
    width_t = teacher_gain.shape[0]
    width_s = norm_gain.shape[0]
    share = student_hidden.shape[1]
    outer_at = lax.axis_index(OUTER)
    inner_at = lax.axis_index(INNER)
    group_at = lax.axis_index(GROUP)

    def to_gathered(w):
        parts = w.reshape((outer // 2, inner, 2, -1) + w.shape[1:])
        return jnp.swapaxes(parts, 0, 1).reshape(w.shape)

    def from_gathered(w):
        parts = w.reshape((inner, outer // 2, 2, -1) + w.shape[1:])
        return jnp.swapaxes(parts, 0, 1).reshape(w.shape)

    teacher_flat = teacher_head.reshape(width_t, level_count * code_count)
    student_flat = student_head.reshape(width_s, level_count * code_count)
    level_mask = (jnp.arange(level_count, dtype=jnp.int32)[:, None] == levels[None, :]).astype(F32)

    teacher_t = lax.all_gather(teacher_hidden.T, OUTER, axis=0, tiled=True)
    teacher_t = lax.all_gather(teacher_t, INNER, axis=0, tiled=True)

    own_cols = student_hidden.T
    student_t = spread(spread(own_cols, OUTER, outer), INNER, inner)
    student_in = student_t.astype(F32)
    scale_in = lax.rsqrt(jnp.mean(student_in * student_in, axis=0) + NORM_EPS)
    gain_in = to_gathered(norm_gain)
    normed_in = (student_in * scale_in[None, :] * gain_in[:, None]).astype(BF16)
    both_weight = to_gathered(jnp.concatenate([gate_weight, up_weight], axis=1))
    both_pre = dot(both_weight, normed_in, 0, 0)
    units = gate_weight.shape[1]
    gate_pre, up_pre = both_pre[:units], both_pre[units:]
    sigma = jax.nn.sigmoid(gate_pre)
    gate_act = gate_pre * sigma
    gate_slope = sigma * (1.0 + gate_pre * (1.0 - sigma))
    hidden = (gate_act * up_pre).astype(BF16)
    down_part = dot(hidden, down_weight, 0, 0).astype(BF16)
    down_own = collect(collect(down_part, INNER, inner).astype(BF16), OUTER, outer)
    own_rows = row_count // (outer * inner)
    row_start = (inner_at * outer + outer_at) * own_rows
    student_own = lax.dynamic_slice_in_dim(student_t, row_start, own_rows, 1).astype(F32)
    mixed_rows = from_gathered(student_own).T + down_own
    scale_out = lax.rsqrt(jnp.mean(mixed_rows * mixed_rows, axis=1) + NORM_EPS)
    normed_own = (mixed_rows * scale_out[:, None] * final_gain).astype(BF16)

    centre_part = jnp.mean(student_head.astype(F32), axis=2).T
    centre_part = jnp.pad(centre_part, ((0, 16 - level_count), (0, 0)))
    sent = spread(jnp.concatenate([normed_own, centre_part.astype(BF16)]), OUTER, outer)
    sent = sent.reshape(outer, -1, width_s)
    centre_part = jnp.mean(sent[:, own_rows:].astype(F32), axis=0)
    sent = jnp.concatenate(
        [sent[:, :own_rows].reshape(-1, width_s), centre_part.astype(BF16)], axis=0
    )
    sent = spread(sent, INNER, inner).reshape(inner, -1, width_s)
    normed_out = sent[:, : outer * own_rows].reshape(row_count, width_s)
    centre = jnp.mean(sent[:, outer * own_rows :].astype(F32), axis=0)[:level_count]
    student_centred = (
        (student_head.astype(F32) - centre.T[:, :, None])
        .astype(BF16)
        .reshape(width_s, level_count * code_count)
    )

    teacher_wide = from_gathered(teacher_t).astype(F32)
    teacher_scale = lax.rsqrt(jnp.mean(teacher_wide * teacher_wide, axis=0) + NORM_EPS)
    teacher_normed = (teacher_wide * teacher_scale[None, :] * teacher_gain[:, None]).astype(BF16)

    def pick_level(all_levels):
        return jnp.sum(
            all_levels.reshape(level_count, code_count, row_count) * level_mask[:, None, :], axis=0
        )

    teacher_logits = pick_level(dot(teacher_flat, teacher_normed, 0, 0))
    student_logits = pick_level(dot(student_flat, normed_out, 0, 1))
    peak_s = jnp.max(student_logits, axis=0)
    peak_t = jnp.max(teacher_logits, axis=0)
    expo_t = jnp.exp(teacher_logits - peak_t)
    total_t = jnp.sum(expo_t, axis=0)
    part_s = peak_s + jnp.log(jnp.sum(jnp.exp(student_logits - peak_s), axis=0))
    part_t = peak_t + jnp.log(total_t)
    part_cross = jnp.sum(expo_t * (teacher_logits - student_logits), axis=0) / total_t
    codes_here = group_at * code_count + jnp.arange(code_count, dtype=jnp.int32)
    part_score = jnp.sum(
        jnp.where(codes_here[:, None] == sampled_codes[None, :], teacher_logits, 0.0), axis=0
    )
    stats = jnp.stack([part_s, part_t, part_cross, part_score])
    stats = spread(stats, GROUP, outer * inner).reshape(outer * inner, 4, row_count)
    norm_s = jax.nn.logsumexp(stats[:, 0], axis=0)
    norm_t = jax.nn.logsumexp(stats[:, 1], axis=0)
    cross = jnp.sum(jnp.exp(stats[:, 1] - norm_t) * stats[:, 2], axis=0)
    token_kl = cross - norm_t + norm_s
    sampled_score = jnp.sum(stats[:, 3], axis=0) - norm_t
    code_grad = jnp.exp(student_logits - norm_s) - jnp.exp(teacher_logits - norm_t)
    grad_full = (
        (level_mask[:, None, :] * code_grad[None])
        .astype(BF16)
        .reshape(level_count * code_count, row_count)
    )

    code_part = dot(grad_full, student_centred, 0, 1).astype(BF16)
    back_out = collect(collect(code_part, INNER, inner).astype(BF16), OUTER, outer)
    head_term = dot(normed_out, grad_full, 0, 1).astype(BF16)
    head_share = lax.psum_scatter(head_term, ROWS, scatter_dimension=0, tiled=True)
    gained = final_gain * back_out
    back_mixed = (
        scale_out[:, None] * gained
        - mixed_rows * (scale_out**3)[:, None] * jnp.mean(gained * mixed_rows, axis=1)[:, None]
    )
    back_mixed_b = spread(spread(back_mixed.astype(BF16), OUTER, outer), INNER, inner)
    back_mixed_b, head_share = lax.optimization_barrier((back_mixed_b, head_share))

    back_hidden = dot(down_weight, back_mixed_b, 1, 1)
    back_both = jnp.concatenate(
        [
            (back_hidden * up_pre * gate_slope).astype(BF16),
            (back_hidden * gate_act).astype(BF16),
        ]
    )
    both_term = from_gathered(dot(normed_in, back_both, 1, 1).astype(BF16))
    down_term = dot(back_mixed_b, hidden, 0, 1).astype(BF16)
    grad_share = lax.psum_scatter(
        jnp.concatenate([both_term, down_term], axis=1), ROWS, scatter_dimension=0, tiled=True
    ).astype(F32)
    gate_share = grad_share[:, :units]
    up_share = grad_share[:, units : 2 * units]
    down_share = grad_share[:, 2 * units :].T

    back_part = dot(both_weight, back_both, 1, 0)
    row_part = jnp.sum(gain_in[:, None] * student_in * back_part, axis=0)

    def with_rows(part, row_term, count):
        high = row_term.astype(BF16)
        low = (row_term - high.astype(F32)).astype(BF16)
        extra = jnp.concatenate(
            [high[None], low[None], jnp.zeros((14, row_count), BF16)], axis=0
        )
        part = part.astype(BF16).reshape(count, -1, row_count)
        extra = jnp.broadcast_to(extra[None], (count, 16, row_count))
        return jnp.concatenate([part, extra], axis=1).reshape(-1, row_count)

    got = collect(with_rows(back_part, row_part, inner), INNER, inner)
    block = outer * share
    got = collect(with_rows(got[:block], got[block] + got[block + 1], outer), OUTER, outer)
    back_in = got[:share]
    row_mean = (got[share] + got[share + 1]) / width_s
    share_start = group_at * share
    back_own = lax.dynamic_slice_in_dim(back_mixed_b, share_start, share, 1).T.astype(F32)
    own_gain = lax.dynamic_slice_in_dim(norm_gain, share_start, share, 0)
    input_grad = (
        back_own
        + scale_in * own_gain[:, None] * back_in
        - own_cols.astype(F32) * (scale_in**3 * row_mean)
    ).T
    head_grad = head_share.astype(F32).reshape(head_share.shape[0], level_count, code_count)
    return (token_kl, sampled_score, head_grad, gate_share, up_share, down_share, input_grad)


def solution(mesh):
    split = Mesh(mesh.devices.reshape(4, 4, 2, 4, 2), ("zh", "x", "core", "y", "zl"))
    placed = (
        P(ROWS, GROUP),
        P(),
        P(None, None, GROUP),
        P(ROWS, GROUP),
        P(),
        P(None, GROUP),
        P(None, GROUP),
        P(GROUP, None),
        P(),
        P(None, None, GROUP),
        P(ROWS),
        P(ROWS),
    )
    return jax.shard_map(
        body,
        mesh=split,
        in_specs=placed,
        out_specs=(
            P(ROWS),
            P(ROWS),
            P(ROWS, None, GROUP),
            P(ROWS, GROUP),
            P(ROWS, GROUP),
            P(GROUP, ROWS),
            P(ROWS, GROUP),
        ),
        check_vma=False,
    )
```
